256 devices in a mesh: blk: 16 (over z, core), cube: 16 (over y, x).
Axes of the slice: x: 4, y: 4, z: 8, core: 2. Of those that a mesh axis runs over, the one named last changes fastest.
Arguments:
- activations: bfloat16 [131072, 8192], P(('blk', 'cube')), may hold values from -16 to 16, as said below
- out_grads: bfloat16 [131072, 512], P(('blk', 'cube')), may hold values from -1 to 1, as said below
Outputs:
- combined: float32 [8192, 512], P('blk', 'cube')
The draws below stay inside these ranges and needn't reach their ends.
Inputs may be any that keep to these rules, and one draw needn't show every extreme that they name: Real-valued activations. `out_grads`: Real-valued output gradients.
All inputs are finite; a program needn't handle non-finite values.
Results may differ from the reference program's by a relative error of at most 0.0003.
Values may be sent and summed in bfloat16 or wider, within the bound.
A program may use at most 128 MiB of HBM per device.

```python
import math
import jax
import jax.numpy as jnp
from jax import lax

D = 8192
KVW = 512
TOK_DEV = 512
CYCLE = 16
GROUPS = 16
LEVELS = 4
TOKENS = 131072


def log_scales(key, amount, top_value):
    uniform_draw = jax.random.uniform(key, (amount,), jnp.float32)
    return jnp.exp(uniform_draw * math.log(top_value))


def noise_field(key, dims_shape):
    return jnp.clip(jax.random.normal(key, dims_shape, jnp.float32), -4.0, 4.0)


def token_matrix(key, extent):
    key_list = jax.random.split(key, 4)
    common_share = 0.5
    end_ratio = 3.0
    top_value = 10.0
    spread = math.sqrt((top_value * top_value - 1.0) / (2.0 * math.log(top_value)))
    ramp_up = jnp.exp(0.5 * math.log(end_ratio) * jnp.arange(extent, dtype=jnp.float32) / extent)
    columns = log_scales(key_list[0], extent, top_value) * ramp_up / spread
    rowscale = log_scales(key_list[1], CYCLE * GROUPS * TOK_DEV, top_value).reshape(CYCLE, GROUPS, TOK_DEV, 1) / spread
    common = noise_field(key_list[2], (CYCLE, 1, TOK_DEV, extent))
    own_part = noise_field(key_list[3], (CYCLE, GROUPS, TOK_DEV, extent))
    mixture = math.sqrt(common_share) * common + math.sqrt(1.0 - common_share) * own_part
    return (mixture * rowscale * columns.reshape(1, 1, 1, extent)).reshape(TOKENS, extent)


def draw_activations(key, part):
    values = token_matrix(jax.random.fold_in(key, 101), D)
    return jnp.clip(values, -16.0, 16.0).astype(jnp.bfloat16)


def draw_out_grads(key, part):
    values = token_matrix(jax.random.fold_in(key, 202), KVW) * float(TOKENS) ** (-0.5)
    return jnp.clip(values, -1.0, 1.0).astype(jnp.bfloat16)


def setup_inputs(seed: int = 0) -> dict:
    seeds = jax.random.split(jax.random.key(seed), 3)
    return {
        "activations": draw_activations(jax.random.fold_in(seeds[2], 71), 0),
        "out_grads": draw_out_grads(jax.random.fold_in(seeds[2], 71), 0),
    }


epsilon = 1e-6


def adasum_pair(former, latter):
    inner_prod = jnp.sum(former * latter)
    former_sq = jnp.sum(former * former)
    latter_sq = jnp.sum(latter * latter)
    return (1.0 - inner_prod / (2.0 * (former_sq + epsilon))) * former + (1.0 - inner_prod / (2.0 * (latter_sq + epsilon))) * latter


def reference(activations, out_grads):
    token_acts = activations.reshape(CYCLE, GROUPS, TOK_DEV, D)
    token_grads = out_grads.reshape(CYCLE, GROUPS, TOK_DEV, KVW)
    vectors = []
    for group_id in range(GROUPS):
        left_rows = token_acts[:, group_id].reshape(CYCLE * TOK_DEV, D)
        right_rows = token_grads[:, group_id].reshape(CYCLE * TOK_DEV, KVW)
        vectors.append(lax.dot_general(left_rows, right_rows, (((0,), (0,)), ((), ())), preferred_element_type=jnp.float32))
    for bit_level in range(LEVELS):
        stride = 2 ** bit_level
        merged = list(vectors)
        for low_index in range(GROUPS):
            if (low_index // stride) % 2 == 0:
                joined = adasum_pair(vectors[low_index], vectors[low_index + stride])
                merged[low_index] = joined
                merged[low_index + stride] = joined
        vectors = merged
    return vectors[0]
```

```python
import jax
import jax.numpy as jnp
from jax import lax
from jax.experimental import pallas as pl
from jax.experimental.pallas import tpu as pltpu
from jax.sharding import PartitionSpec as P

MESH = pl.DeviceIdType.MESH
EPS = 1e-6
NZ = 8
NG = 16
STEPS = NZ - 1
F32, BF16 = jnp.float32, jnp.bfloat16
SLOTS = (7, 1, 6, 2, 5, 3, 4, 0)


def kernel(
    a_hbm, g_hbm, out_ref,
    av, gv, gt, hs, hr, ls, lr, xs, xr, zs, zr, ks, kz, kc,
    own_sem, par_send, par_recv, hi_send, hi_recv, lo_send, lo_recv,
    x_send, x_recv, z_send, z_recv, k_send, k_recv,
):
    b = lax.axis_index("blk")
    g = lax.axis_index("cube")
    z, core = b >> 1, b & 1
    y, x = g >> 2, g & 3
    partner = (b ^ 1, g)
    ring = (
        (((z + 1) & 7) * 2 + core, g),
        (((z + 7) & 7) * 2 + core, g),
    )
    plane = []
    for k in range(1, NG):
        plane.append((((y + k // 4) & 3) * 4) + ((x + k % 4) & 3))
    line = [b ^ j for j in range(1, NG)]
    tok = a_hbm.shape[0]
    bw = a_hbm.shape[1] // (2 * NZ)
    half = bw // 2
    kv = g_hbm.shape[1]
    kvh = kv // 2
    ks_rows = kv // NG

    barrier = pltpu.get_barrier_semaphore()
    for p in line:
        pl.semaphore_signal(barrier, inc=1, device_id=(p, g), device_id_type=MESH)
    for p in plane:
        pl.semaphore_signal(barrier, inc=1, device_id=(b, p), device_id_type=MESH)

    def block(slot, parity):
        start = (((z + slot) & 7) * 2 + parity) * bw
        return a_hbm.at[:, pl.ds(pl.multiple_of(start, bw), bw)]

    own = [pltpu.make_async_copy(g_hbm, gv.at[pl.ds(0, tok)], own_sem.at[NZ])]
    own[0].start()
    for s in range(NZ):
        own.append(pltpu.make_async_copy(block(s, core), av.at[s, pl.ds(0, tok)], own_sem.at[s]))
    for s in SLOTS:
        own[s + 1].start()

    pl.semaphore_wait(barrier, 2 * (NG - 1))

    def remote(src, dst, send, recv, dev):
        return pltpu.make_async_remote_copy(
            src_ref=src, dst_ref=dst, send_sem=send, recv_sem=recv, device_id=dev, device_id_type=MESH
        )

    par = [remote(g_hbm, gv.at[pl.ds(tok, tok)], par_send.at[NZ], par_recv.at[NZ], partner)]
    par[0].start()
    for s in range(NZ):
        par.append(
            remote(block(s, 1 - core), av.at[s, pl.ds(tok, tok)], par_send.at[s], par_recv.at[s], partner)
        )
    for s in SLOTS:
        par[s + 1].start()

    own[0].wait()
    gt[:, :tok] = gv[:tok, :].T
    par[0].wait_recv()
    gt[:, tok:] = gv[tok:, :].T

    waited = set()

    def ready(slot):
        if slot not in waited:
            waited.add(slot)
            own[slot + 1].wait()
            par[slot + 1].wait_recv()

    def share(slot, way, h):
        return jnp.dot(
            gt[way * kvh : (way + 1) * kvh, :],
            av[slot, :, h * half : (h + 1) * half],
            preferred_element_type=F32,
        )

    def hop(t, way, h):
        return remote(hs.at[t, way, h], hr.at[t, way, h], hi_send.at[t, way, h], hi_recv.at[t, way, h], ring[way])

    def spread(src, dst, send, recv):
        for p in plane:
            remote(src.at[p], dst.at[g], send, recv, (b, p)).start()
        pltpu.make_async_copy(src.at[g], dst.at[g], recv).start()

    def spread_wait_recv(dst, recv):
        pltpu.make_async_copy(dst, dst, recv).wait()

    def spread_wait_send(src, send):
        part = src.at[pl.ds(0, NG - 1)]
        pltpu.make_async_copy(part, part, send).wait()

    for t in range(STEPS + 1):
        for h in range(2):
            for way in range(2):
                if t == STEPS:
                    slot = 0
                else:
                    slot = NZ - 1 - t if way == 0 else 1 + t
                ready(slot)
                total = share(slot, way, h)
                if t > 0:
                    hop(t - 1, way, h).wait_recv()
                    total = total + hr[t - 1, way, h].astype(F32)
                hi = total.astype(BF16)
                if t < STEPS:
                    hs[t, way, h] = hi
                    hop(t, way, h).start()
                else:
                    xs[h, way * 8 : way * 8 + 8] = hi.reshape(8, ks_rows, half)
                lo = (total - hi.astype(F32)).astype(BF16)
                ls[t, way * 8 : way * 8 + 8, :, h * half : (h + 1) * half] = lo.reshape(8, ks_rows, half)
            if t == STEPS:
                spread(xs.at[h], xr.at[h], x_send.at[h], x_recv.at[h])
        spread(ls.at[t], lr.at[t], lo_send.at[t], lo_recv.at[t])

    gram = None
    for h in range(2):
        spread_wait_recv(xr.at[h], x_recv.at[h])
        rows = xr[h].reshape(kv, half)
        part = lax.dot_general(rows, rows, (((1,), (1,)), ((), ())), preferred_element_type=F32)
        gram = part if gram is None else gram + part
    same = (lax.broadcasted_iota(jnp.int32, (kv, kv), 0) & (ks_rows - 1)) == (
        lax.broadcasted_iota(jnp.int32, (kv, kv), 1) & (ks_rows - 1)
    )
    gram = jnp.where(same, gram, 0.0).reshape(NG, ks_rows, kv).sum(axis=1)
    pick = (lax.broadcasted_iota(jnp.int32, (kv, 128), 0) >> 5) == lax.broadcasted_iota(jnp.int32, (kv, 128), 1)
    gram = jnp.dot(gram, pick.astype(F32), precision=lax.Precision.HIGHEST, preferred_element_type=F32)

    ks[0] = gram
    kz[b] = gram
    for p in line:
        remote(ks.at[0], kz.at[b], k_send.at[0], k_recv.at[0], (p, g)).start()
    most = pl.ds(0, NG - 1)
    pltpu.make_async_copy(kz.at[most], kz.at[most], k_recv.at[0]).wait()
    gram = kz[...].sum(axis=0)
    ks[1] = gram
    kc[g] = gram
    for p in plane:
        remote(ks.at[1], kc.at[g], k_send.at[1], k_recv.at[1], (b, p)).start()
    pltpu.make_async_copy(kc.at[most], kc.at[most], k_recv.at[1]).wait()
    gram = kc[...].sum(axis=0)

    row = lax.broadcasted_iota(jnp.int32, (NG, 128), 0)
    col = lax.broadcasted_iota(jnp.int32, (NG, 128), 1)
    coef = jnp.ones((NG, 1), F32)
    for level in range(4):
        bit = 1 << level
        diag = jnp.where(row == col, gram, 0.0)
        cross = jnp.where((row ^ bit) == col, gram, 0.0)

        def factor(axis):
            sq = jnp.maximum(jnp.sum(diag, axis=axis, keepdims=True), 0.0)
            return 1.0 - jnp.sum(cross, axis=axis, keepdims=True) / (2.0 * (sq + EPS))

        by_row, by_col = factor(1), factor(0)
        coef = coef * by_row
        gram = gram * by_row * by_col
        gram = gram + jnp.where((row & bit) != 0, pltpu.roll(gram, bit, 0), pltpu.roll(gram, NG - bit, 0))
        gram = gram + jnp.where((col & bit) != 0, pltpu.roll(gram, bit, 1), pltpu.roll(gram, 128 - bit, 1))
    coef = jnp.broadcast_to(coef, (NG, 128))

    def combine(ref):
        width = ref.shape[-1]
        acc = jnp.zeros((ks_rows, width), F32)
        for i in range(NG):
            acc = acc + jnp.tile(coef[i : i + 1], (1, width // 128)) * ref[i].astype(F32)
        return acc

    side = 2 * (g >> 3) - 1
    home = []
    for t in range(STEPS):
        spread_wait_recv(lr.at[t], lo_recv.at[t])
        zs[t] = combine(lr.at[t]).astype(BF16)
        dest = (z + (1 + t) * side + 8) & 7
        home.append(remote(zs.at[t], zr.at[t], z_send.at[t], z_recv.at[t], (dest * 2 + core, g)))
        home[t].start()
    spread_wait_recv(lr.at[STEPS], lo_recv.at[STEPS])
    acc = combine(lr.at[STEPS])
    acc = acc + jnp.concatenate([combine(xr.at[0]), combine(xr.at[1])], axis=1)
    for t in range(STEPS):
        home[t].wait_recv()
        acc = acc + zr[t].astype(F32)
    out_ref[...] = acc

    for s in range(NZ + 1):
        par[s].wait_send()
    for t in range(STEPS):
        home[t].wait_send()
        for way in range(2):
            for h in range(2):
                hop(t, way, h).wait_send()
    for t in range(STEPS + 1):
        spread_wait_send(ls.at[t], lo_send.at[t])
    for h in range(2):
        spread_wait_send(xs.at[h], x_send.at[h])
    for s in range(2):
        pltpu.make_async_copy(kz.at[most], kz.at[most], k_send.at[s]).wait()


def shards(activations, out_grads):
    tok, d = activations.shape
    kv = out_grads.shape[1]
    bw = d // (2 * NZ)
    half = bw // 2
    rows = kv // NG
    dma = pltpu.SemaphoreType.DMA
    grad = pl.pallas_call(
        kernel,
        out_shape=jax.ShapeDtypeStruct((rows, bw), F32),
        in_specs=[pl.BlockSpec(memory_space=pl.ANY)] * 2,
        out_specs=pl.BlockSpec(memory_space=pltpu.VMEM),
        scratch_shapes=[
            pltpu.VMEM((NZ, 2 * tok, bw), BF16),
            pltpu.VMEM((2 * tok, kv), BF16),
            pltpu.VMEM((kv, 2 * tok), BF16),
            pltpu.VMEM((STEPS, 2, 2, kv // 2, half), BF16),
            pltpu.VMEM((STEPS, 2, 2, kv // 2, half), BF16),
            pltpu.VMEM((NZ, NG, rows, bw), BF16),
            pltpu.VMEM((NZ, NG, rows, bw), BF16),
            pltpu.VMEM((2, NG, rows, half), BF16),
            pltpu.VMEM((2, NG, rows, half), BF16),
            pltpu.VMEM((STEPS, rows, bw), BF16),
            pltpu.VMEM((STEPS, rows, bw), BF16),
            pltpu.VMEM((2, NG, 128), F32),
            pltpu.VMEM((NG, NG, 128), F32),
            pltpu.VMEM((NG, NG, 128), F32),
            dma((NZ + 1,)),
            dma((NZ + 1,)),
            dma((NZ + 1,)),
            dma((STEPS, 2, 2)),
            dma((STEPS, 2, 2)),
            dma((NZ,)),
            dma((NZ,)),
            dma((2,)),
            dma((2,)),
            dma((STEPS,)),
            dma((STEPS,)),
            dma((2,)),
            dma((2,)),
        ],
        compiler_params=pltpu.CompilerParams(
            collective_id=0, has_side_effects=True, vmem_limit_bytes=56 << 20
        ),
        cost_estimate=pl.CostEstimate(
            flops=2 * tok * d * kv, bytes_accessed=2 * tok * (d + kv), transcendentals=0
        ),
        name="adasum",
    )(activations, out_grads)
    return grad.T


def solution(mesh):
    placed = (P(("blk", "cube"), None), P(("blk", "cube"), None))
    return jax.shard_map(
        shards, mesh=mesh, in_specs=placed, out_specs=P("blk", "cube"), check_vma=False
    )
```

```python
import jax
import jax.numpy as jnp
from jax import lax
from jax.experimental import pallas as pl
from jax.experimental.pallas import tpu as pltpu
from jax.sharding import PartitionSpec as P

MESH = pl.DeviceIdType.MESH
EPS = 1e-6
NZ = 8
NG = 16
STEPS = NZ - 1
F32, BF16 = jnp.float32, jnp.bfloat16
SLOTS = (7, 1, 6, 2, 5, 3, 4, 0)


def kernel(
    a_hbm, g_hbm, out_ref,
    av, gv, gt, hs, hr, ls, lr, ts, tr, rest, xs, xr, zs, zr, ks, kz, kc,
    own_sem, par_send, par_recv, hi_send, hi_recv, lo_send, lo_recv, t_send, t_recv,
    x_send, x_recv, z_send, z_recv, k_send, k_recv, near_sem, far_sem,
):
    b = lax.axis_index("blk")
    g = lax.axis_index("cube")
    z, core = b >> 1, b & 1
    y, x = g >> 2, g & 3
    tok = a_hbm.shape[0]
    bw = a_hbm.shape[1] // (2 * NZ)
    half = bw // 2
    kv = g_hbm.shape[1]
    kvh = kv // 2
    ks_rows = kv // NG
    last = STEPS - 1

    def at_plane(dy, dx):
        return (((y + dy) & 3) * 4) + ((x + dx) & 3)

    partner = (b ^ 1, g)
    ring = ((((z + 1) & 7) * 2 + core, g), (((z + 7) & 7) * 2 + core, g))
    plane = [
        at_plane(dy, dx)
        for dy, dx in sorted(
            ((dy, dx) for dy in range(4) for dx in range(4) if dy or dx),
            key=lambda o: -(min(o[0], 4 - o[0]) + min(o[1], 4 - o[1])),
        )
    ]
    line = [(((z + dz) & 7) * 2 + core, g) for dz in (4, 3, 5, 2, 6, 1, 7)]
    beside = [(b, at_plane(dy, dx)) for dy, dx in ((0, 1), (0, 3), (1, 0), (3, 0))]
    across = [(b, at_plane(dy, dx)) for dy, dx in ((0, 2), (2, 0))]

    own = [pltpu.make_async_copy(g_hbm, gv, own_sem.at[NZ])]
    own[0].start()

    barrier = pltpu.get_barrier_semaphore()
    near = [partner, *ring, *beside]
    for p in near:
        pl.semaphore_signal(barrier, inc=1, device_id=p, device_id_type=MESH)

    def block(slot, parity):
        start = (((z + slot) & 7) * 2 + parity) * bw
        return a_hbm.at[:, pl.ds(pl.multiple_of(start, bw), bw)]

    for s in range(NZ):
        own.append(pltpu.make_async_copy(block(s, core), av.at[s, pl.ds(0, tok)], own_sem.at[s]))
    for s in SLOTS[:2]:
        own[s + 1].start()

    own[0].wait()
    gt[:, :tok] = gv[...].T
    pl.semaphore_wait(barrier, len(near))

    def remote(src, dst, send, recv, dev):
        return pltpu.make_async_remote_copy(
            src_ref=src, dst_ref=dst, send_sem=send, recv_sem=recv, device_id=dev, device_id_type=MESH
        )

    def par(slot, h):
        return remote(
            block(slot, 1 - core).at[:, pl.ds(h * half, half)],
            av.at[slot, pl.ds(tok, tok), pl.ds(h * half, half)],
            par_send.at[slot, h], par_recv.at[slot, h], partner,
        )

    def par_grad(way):
        rows = pl.ds(way * kvh, kvh)
        return remote(
            gt.at[rows, pl.ds(0, tok)], gt.at[rows, pl.ds(tok, tok)], par_send.at[NZ, way], par_recv.at[NZ, way], partner
        )

    for h in range(2):
        for way in range(2):
            if h == 0:
                par_grad(way).start()
            par(SLOTS[way], h).start()

    def fetch(slots):
        for s in slots:
            own[s + 1].start()
            for h in range(2):
                par(s, h).start()

    for p in beside:
        pl.semaphore_signal(near_sem, inc=1, device_id=p, device_id_type=MESH)

    waited = set()

    def ready(way, slot, h):
        if ("grad", way) not in waited:
            waited.add(("grad", way))
            par_grad(way).wait_recv()
        if slot not in waited:
            waited.add(slot)
            own[slot + 1].wait()
        if (slot, h) not in waited:
            waited.add((slot, h))
            par(slot, h).wait_recv()

    def share(slot, way, h):
        return jnp.dot(
            gt[way * kvh : (way + 1) * kvh, :],
            av[slot, :, h * half : (h + 1) * half],
            preferred_element_type=F32,
        )

    def hop(t, way, h):
        return remote(hs.at[t, way, h], hr.at[t, way, h], hi_send.at[t, way, h], hi_recv.at[t, way, h], ring[way])

    def trail(way, h):
        return remote(ts.at[way, h], tr.at[way, h], t_send.at[way, h], t_recv.at[way, h], ring[way])

    def parts(src, dst, send, recv):
        return [remote(src.at[p], dst.at[g], send, recv, (b, p)) for p in plane] + [
            pltpu.make_async_copy(src.at[g], dst.at[g], recv)
        ]

    def spread(src, dst, send, recv):
        for copy in parts(src, dst, send, recv):
            copy.start()

    def spread_wait_recv(dst, recv):
        pltpu.make_async_copy(dst, dst, recv).wait()

    def spread_wait_send(src, send):
        part = src.at[pl.ds(0, NG - 1)]
        pltpu.make_async_copy(part, part, send).wait()

    queue = []
    for t in range(STEPS + 1):
        for h in range(2):
            for way in range(2):
                if t == STEPS:
                    slot = 0
                else:
                    slot = NZ - 1 - t if way == 0 else 1 + t
                ready(way, slot, h)
                total = share(slot, way, h)
                if t > 0:
                    hop(t - 1, way, h).wait_recv()
                    total = total + hr[t - 1, way, h].astype(F32)
                hi = total.astype(BF16)
                if t < STEPS:
                    hs[t, way, h] = hi
                    hop(t, way, h).start()
                else:
                    xs[h, way * 8 : way * 8 + 8] = hi.reshape(8, ks_rows, half)
                lo = total - hi.astype(F32)
                if t < last:
                    ls[t, way * 8 : way * 8 + 8, :, h * half : (h + 1) * half] = lo.astype(BF16).reshape(8, ks_rows, half)
                elif t == last:
                    ts[way, h] = lo.astype(BF16)
                else:
                    rest[way, h] = lo
                for copy in queue[:4]:
                    copy.start()
                queue = queue[4:]
            if t == STEPS:
                spread(xs.at[h], xr.at[h], x_send.at[h], x_recv.at[h])
        fetch(SLOTS[2 * t + 2 : 2 * t + 4])
        if t == 0:
            pl.semaphore_wait(near_sem, len(beside))
            for p in across:
                pl.semaphore_signal(far_sem, inc=1, device_id=p, device_id_type=MESH)
            pl.semaphore_wait(far_sem, len(across))
        if t < last:
            queue = parts(ls.at[t], lr.at[t], lo_send.at[t], lo_recv.at[t])
        elif t == last:
            for h in range(2):
                for way in range(2):
                    trail(way, h).start()

    gram = None
    for h in range(2):
        spread_wait_recv(xr.at[h], x_recv.at[h])
        rows = xr[h].reshape(kv, half)
        part = lax.dot_general(rows, rows, (((1,), (1,)), ((), ())), preferred_element_type=F32)
        gram = part if gram is None else gram + part
    same = (lax.broadcasted_iota(jnp.int32, (kv, kv), 0) & (ks_rows - 1)) == (
        lax.broadcasted_iota(jnp.int32, (kv, kv), 1) & (ks_rows - 1)
    )
    gram = jnp.where(same, gram, 0.0).reshape(NG, ks_rows, kv).sum(axis=1)
    pick = (lax.broadcasted_iota(jnp.int32, (kv, 128), 0) >> 5) == lax.broadcasted_iota(jnp.int32, (kv, 128), 1)
    gram = jnp.dot(gram, pick.astype(F32), precision=lax.Precision.HIGHEST, preferred_element_type=F32)

    most = pl.ds(0, NG - 1)
    ks[0] = gram
    kc[g] = gram
    for p in plane:
        remote(ks.at[0], kc.at[g], k_send.at[0], k_recv.at[0], (b, p)).start()
    for h in range(2):
        for way in range(2):
            trail(way, h).wait_recv()
            lo = rest[way, h] + tr[way, h].astype(F32)
            ls[last, way * 8 : way * 8 + 8, :, h * half : (h + 1) * half] = lo.astype(BF16).reshape(8, ks_rows, half)
    pltpu.make_async_copy(kc.at[most], kc.at[most], k_recv.at[0]).wait()
    gram = kc[...].sum(axis=0)
    ks[1] = gram
    swap = remote(ks.at[1], kz.at[NZ], k_send.at[1], k_recv.at[1], partner)
    swap.start()
    swap.wait_recv()
    gram = gram + kz[NZ]
    ks[2] = gram
    kz[z] = gram
    for p in line:
        remote(ks.at[2], kz.at[z], k_send.at[2], k_recv.at[2], p).start()
    spread(ls.at[last], lr.at[last], lo_send.at[last], lo_recv.at[last])
    ahead = pl.ds(0, NZ - 1)
    pltpu.make_async_copy(kz.at[ahead], kz.at[ahead], k_recv.at[2]).wait()
    gram = kz[:NZ].sum(axis=0)

    row = lax.broadcasted_iota(jnp.int32, (NG, 128), 0)
    col = lax.broadcasted_iota(jnp.int32, (NG, 128), 1)
    coef = jnp.ones((NG, 1), F32)
    for level in range(4):
        bit = 1 << level
        diag = jnp.where(row == col, gram, 0.0)
        cross = jnp.where((row ^ bit) == col, gram, 0.0)

        def factor(axis):
            sq = jnp.maximum(jnp.sum(diag, axis=axis, keepdims=True), 0.0)
            return 1.0 - jnp.sum(cross, axis=axis, keepdims=True) / (2.0 * (sq + EPS))

        by_row, by_col = factor(1), factor(0)
        coef = coef * by_row
        gram = gram * by_row * by_col
        gram = gram + jnp.where((row & bit) != 0, pltpu.roll(gram, bit, 0), pltpu.roll(gram, NG - bit, 0))
        gram = gram + jnp.where((col & bit) != 0, pltpu.roll(gram, bit, 1), pltpu.roll(gram, 128 - bit, 1))
    coef = jnp.broadcast_to(coef, (NG, 128))

    def combine(ref):
        width = ref.shape[-1]
        acc = jnp.zeros((ks_rows, width), F32)
        for i in range(NG):
            acc = acc + jnp.tile(coef[i : i + 1], (1, width // 128)) * ref[i].astype(F32)
        return acc

    side = 2 * (g >> 3) - 1

    def home(t):
        dest = (z + (1 + t) * side + 8) & 7
        return remote(zs.at[t], zr.at[t], z_send.at[t], z_recv.at[t], (dest * 2 + core, g))

    for t in (3, 2, 4, 1, 5, 0):
        spread_wait_recv(lr.at[t], lo_recv.at[t])
        zs[t] = combine(lr.at[t]).astype(BF16)
        home(t).start()
    acc = jnp.concatenate([combine(xr.at[0]), combine(xr.at[1])], axis=1)
    spread_wait_recv(lr.at[last], lo_recv.at[last])
    acc = acc + combine(lr.at[last])
    for t in (0, 5, 1, 4, 2, 3):
        home(t).wait_recv()
        acc = acc + zr[t].astype(F32)
    out_ref[...] = acc

    for way in range(2):
        par_grad(way).wait_send()
        for h in range(2):
            for s in range(way * 4, way * 4 + 4):
                par(s, h).wait_send()
            for t in range(STEPS):
                hop(t, way, h).wait_send()
            trail(way, h).wait_send()
    for t in range(STEPS):
        spread_wait_send(ls.at[t], lo_send.at[t])
    for t in range(last):
        home(t).wait_send()
    for h in range(2):
        spread_wait_send(xs.at[h], x_send.at[h])
    pltpu.make_async_copy(kc.at[most], kc.at[most], k_send.at[0]).wait()
    swap.wait_send()
    pltpu.make_async_copy(kz.at[ahead], kz.at[ahead], k_send.at[2]).wait()


def shards(activations, out_grads):
    tok, d = activations.shape
    kv = out_grads.shape[1]
    bw = d // (2 * NZ)
    half = bw // 2
    rows = kv // NG
    dma = pltpu.SemaphoreType.DMA
    grad = pl.pallas_call(
        kernel,
        out_shape=jax.ShapeDtypeStruct((rows, bw), F32),
        in_specs=[pl.BlockSpec(memory_space=pl.ANY)] * 2,
        out_specs=pl.BlockSpec(memory_space=pltpu.VMEM),
        scratch_shapes=[
            pltpu.VMEM((NZ, 2 * tok, bw), BF16),
            pltpu.VMEM((tok, kv), BF16),
            pltpu.VMEM((kv, 2 * tok), BF16),
            pltpu.VMEM((STEPS, 2, 2, kv // 2, half), BF16),
            pltpu.VMEM((STEPS, 2, 2, kv // 2, half), BF16),
            pltpu.VMEM((STEPS, NG, rows, bw), BF16),
            pltpu.VMEM((STEPS, NG, rows, bw), BF16),
            pltpu.VMEM((2, 2, kv // 2, half), BF16),
            pltpu.VMEM((2, 2, kv // 2, half), BF16),
            pltpu.VMEM((2, 2, kv // 2, half), F32),
            pltpu.VMEM((2, NG, rows, half), BF16),
            pltpu.VMEM((2, NG, rows, half), BF16),
            pltpu.VMEM((STEPS - 1, rows, bw), BF16),
            pltpu.VMEM((STEPS - 1, rows, bw), BF16),
            pltpu.VMEM((3, NG, 128), F32),
            pltpu.VMEM((NZ + 1, NG, 128), F32),
            pltpu.VMEM((NG, NG, 128), F32),
            dma((NZ + 1,)),
            dma((NZ + 1, 2)),
            dma((NZ + 1, 2)),
            dma((STEPS, 2, 2)),
            dma((STEPS, 2, 2)),
            dma((STEPS,)),
            dma((STEPS,)),
            dma((2, 2)),
            dma((2, 2)),
            dma((2,)),
            dma((2,)),
            dma((STEPS - 1,)),
            dma((STEPS - 1,)),
            dma((3,)),
            dma((3,)),
            pltpu.SemaphoreType.REGULAR,
            pltpu.SemaphoreType.REGULAR,
        ],
        compiler_params=pltpu.CompilerParams(
            collective_id=0, has_side_effects=True, vmem_limit_bytes=56 << 20
        ),
        cost_estimate=pl.CostEstimate(
            flops=2 * tok * d * kv, bytes_accessed=2 * tok * (d + kv), transcendentals=0
        ),
        name="adasum",
    )(activations, out_grads)
    return grad.T


def solution(mesh):
    placed = (P(("blk", "cube"), None), P(("blk", "cube"), None))
    return jax.shard_map(
        shards, mesh=mesh, in_specs=placed, out_specs=P("blk", "cube"), check_vma=False
    )
```

```python
import jax
import jax.numpy as jnp
from jax import lax
from jax.experimental import pallas as pl
from jax.experimental.pallas import tpu as pltpu
from jax.sharding import PartitionSpec as P

MESH = pl.DeviceIdType.MESH
EPS = 1e-6
NZ = 8
NG = 16
STEPS = NZ - 1
F32, BF16 = jnp.float32, jnp.bfloat16
SLOTS = (7, 1, 6, 2, 0, 5, 3, 4)
CHUNKS = ((0, 256), (256, 256))
NC = len(CHUNKS)


def kernel(
    a_hbm, g_hbm, out_ref,
    av, gv, gt, hs, hr, ls, lr, ts, tr, rest, ps, pr, rr, xs, xr, zs, zr, ks, kz, kc,
    own_sem, par_send, par_recv, hi_send, hi_recv, lo_send, lo_recv, t_send, t_recv,
    p_send, p_recv, x_send, x_recv, z_send, z_recv, k_send, k_recv, near_sem, far_sem,
):
    b = lax.axis_index("blk")
    g = lax.axis_index("cube")
    z, core = b >> 1, b & 1
    y, x = g >> 2, g & 3
    tok = a_hbm.shape[0]
    bw = a_hbm.shape[1] // (2 * NZ)
    kv = g_hbm.shape[1]
    kvh = kv // 2
    ks_rows = kv // NG
    last = STEPS - 1

    def at_plane(dy, dx):
        return (((y + dy) & 3) * 4) + ((x + dx) & 3)

    partner = (b ^ 1, g)
    ring = ((((z + 1) & 7) * 2 + core, g), (((z + 7) & 7) * 2 + core, g))
    plane = [
        at_plane(dy, dx)
        for dy, dx in sorted(
            ((dy, dx) for dy in range(4) for dx in range(4) if dy or dx),
            key=lambda o: -(min(o[0], 4 - o[0]) + min(o[1], 4 - o[1])),
        )
    ]
    line = [(((z + dz) & 7) * 2 + core, g) for dz in (4, 3, 5, 2, 6, 1, 7)]
    beside = [(b, at_plane(dy, dx)) for dy, dx in ((0, 1), (0, 3), (1, 0), (3, 0))]
    across = [(b, at_plane(dy, dx)) for dy, dx in ((0, 2), (2, 0))]

    own = [pltpu.make_async_copy(g_hbm, gv, own_sem.at[NZ])]
    own[0].start()

    barrier = pltpu.get_barrier_semaphore()
    near = [partner, *ring, *beside]
    for p in near:
        pl.semaphore_signal(barrier, inc=1, device_id=p, device_id_type=MESH)

    def block(slot, parity):
        start = (((z + slot) & 7) * 2 + parity) * bw
        return a_hbm.at[:, pl.ds(pl.multiple_of(start, bw), bw)]

    for s in range(NZ):
        own.append(pltpu.make_async_copy(block(s, core), av.at[s, pl.ds(0, tok)], own_sem.at[s]))
    for s in SLOTS[:2]:
        own[s + 1].start()

    own[0].wait()
    gt[:, :tok] = gv[...].T
    pl.semaphore_wait(barrier, len(near))

    def remote(src, dst, send, recv, dev):
        return pltpu.make_async_remote_copy(
            src_ref=src, dst_ref=dst, send_sem=send, recv_sem=recv, device_id=dev, device_id_type=MESH
        )

    def cols(h):
        return pl.ds(*CHUNKS[h])

    def par(slot, h):
        return remote(
            block(slot, 1 - core).at[:, cols(h)], av.at[slot, pl.ds(tok, tok), cols(h)],
            par_send.at[slot, h], par_recv.at[slot, h], partner,
        )

    def par_grad(way):
        rows = pl.ds(way * kvh, kvh)
        return remote(
            gt.at[rows, pl.ds(0, tok)], gt.at[rows, pl.ds(tok, tok)], par_send.at[NZ, way], par_recv.at[NZ, way], partner
        )

    for way in range(2):
        par_grad(way).start()
        par(SLOTS[way], 0).start()

    def fetch(slots):
        for s in slots:
            own[s + 1].start()
            for h in range(NC):
                par(s, h).start()

    for p in beside:
        pl.semaphore_signal(near_sem, inc=1, device_id=p, device_id_type=MESH)

    waited = set()

    def ready(way, slot, h):
        if ("grad", way) not in waited:
            waited.add(("grad", way))
            par_grad(way).wait_recv()
        if slot not in waited:
            waited.add(slot)
            own[slot + 1].wait()
        if (slot, h) not in waited:
            waited.add((slot, h))
            par(slot, h).wait_recv()

    def share(slot, way, h):
        return jnp.dot(
            gt[way * kvh : (way + 1) * kvh, :],
            av[slot, :, cols(h)],
            preferred_element_type=F32,
        )

    def hop(t, way, h):
        return remote(
            hs.at[t, way, :, cols(h)], hr.at[t, way, :, cols(h)], hi_send.at[t, way, h], hi_recv.at[t, way, h], ring[way]
        )

    def trail(way):
        return remote(ts.at[way], tr.at[way], t_send.at[way], t_recv.at[way], ring[way])

    def parts(src, dst, send, recv):
        return [remote(src.at[p], dst.at[g], send, recv, (b, p)) for p in plane] + [
            pltpu.make_async_copy(src.at[g], dst.at[g], recv)
        ]

    def spread(src, dst, send, recv, part):
        for p in plane:
            remote(src.at[p, :, part], dst.at[g, :, part], send, recv, (b, p)).start()
        pltpu.make_async_copy(src.at[g, :, part], dst.at[g, :, part], recv).start()

    def spread_wait_recv(dst, recv):
        pltpu.make_async_copy(dst, dst, recv).wait()

    def spread_wait_send(src, send):
        part = src.at[pl.ds(0, NG - 1)]
        pltpu.make_async_copy(part, part, send).wait()

    def slices(value, h):
        return value.reshape(8, ks_rows, CHUNKS[h][1])

    queue = []
    for t in range(STEPS):
        for h in range(NC):
            for way in range(2):
                if t == 0 and h > 0:
                    par(SLOTS[way], h).start()
            for way in range(2):
                slot = NZ - 1 - t if way == 0 else 1 + t
                mine = slice(way * 8, way * 8 + 8)
                ready(way, slot, h)
                total = share(slot, way, h)
                if t > 0:
                    hop(t - 1, way, h).wait_recv()
                    total = total + hr[t - 1, way, :, cols(h)].astype(F32)
                hi = total.astype(BF16)
                if t < last:
                    hs[t, way, :, cols(h)] = hi
                    hop(t, way, h).start()
                else:
                    xs[mine, :, cols(h)] = slices(hi, h)
                    for p in range(way * 8, way * 8 + 8):
                        remote(
                            xs.at[p, :, cols(h)], xr.at[g, :, cols(h)], x_send.at[h], x_recv.at[h], (ring[way][0], p)
                        ).start()
                lo = (total - hi.astype(F32)).astype(BF16)
                if t < last:
                    ls[t, mine, :, cols(h)] = slices(lo, h)
                else:
                    ts[way, :, cols(h)] = lo
                for copy in queue[:5]:
                    copy.start()
                queue = queue[5:]
        if t == 0:
            fetch(SLOTS[2:5])
            pl.semaphore_wait(near_sem, len(beside))
            for p in across:
                pl.semaphore_signal(far_sem, inc=1, device_id=p, device_id_type=MESH)
            pl.semaphore_wait(far_sem, len(across))
        elif t == 1:
            fetch(SLOTS[5:])
            for h in range(NC):
                for way in range(2):
                    ready(way, 0, h)
                    total = share(0, way, h)
                    hi = total.astype(BF16)
                    ps[way * 8 : way * 8 + 8, :, cols(h)] = slices(hi, h)
                    rest[way, :, cols(h)] = total - hi.astype(F32)
            queue = queue + parts(ps, pr, p_send.at[0], p_recv.at[0])
        if t < last - 1:
            queue = queue + parts(ls.at[t], lr.at[t], lo_send.at[t], lo_recv.at[t])
        elif t == last:
            for way in range(2):
                trail(way).start()

    gram = None
    spread_wait_recv(pr, p_recv.at[0])
    for h in range(NC):
        spread_wait_recv(xr.at[:, :, cols(h)], x_recv.at[h])
        whole = xr[:, :, cols(h)].astype(F32) + pr[:, :, cols(h)].astype(F32)
        rr[:, :, cols(h)] = whole
        rows = whole.astype(BF16).reshape(kv, CHUNKS[h][1])
        part = lax.dot_general(rows, rows, (((1,), (1,)), ((), ())), preferred_element_type=F32)
        gram = part if gram is None else gram + part
    same = (lax.broadcasted_iota(jnp.int32, (kv, kv), 0) & (ks_rows - 1)) == (
        lax.broadcasted_iota(jnp.int32, (kv, kv), 1) & (ks_rows - 1)
    )
    gram = jnp.where(same, gram, 0.0).reshape(NG, ks_rows, kv).sum(axis=1)
    pick = (lax.broadcasted_iota(jnp.int32, (kv, 128), 0) >> 5) == lax.broadcasted_iota(jnp.int32, (kv, 128), 1)
    gram = jnp.dot(gram, pick.astype(F32), precision=lax.Precision.HIGHEST, preferred_element_type=F32)

    most = pl.ds(0, NG - 1)
    ks[0] = gram
    kc[g] = gram
    for p in plane:
        remote(ks.at[0], kc.at[g], k_send.at[0], k_recv.at[0], (b, p)).start()
    for way in range(2):
        trail(way).wait_recv()
        lo = rest[way] + tr[way].astype(F32)
        ls[last, way * 8 : way * 8 + 8] = lo.astype(BF16).reshape(8, ks_rows, bw)
    pltpu.make_async_copy(kc.at[most], kc.at[most], k_recv.at[0]).wait()
    gram = kc[...].sum(axis=0)
    ks[1] = gram
    swap = remote(ks.at[1], kz.at[NZ], k_send.at[1], k_recv.at[1], partner)
    swap.start()
    late = last - 1
    spread(ls.at[late], lr.at[late], lo_send.at[late], lo_recv.at[late], slice(None))
    swap.wait_recv()
    gram = gram + kz[NZ]
    ks[2] = gram
    kz[z] = gram
    for p in line:
        remote(ks.at[2], kz.at[z], k_send.at[2], k_recv.at[2], p).start()
    spread(ls.at[last], lr.at[last], lo_send.at[last], lo_recv.at[last], slice(None))
    ahead = pl.ds(0, NZ - 1)
    pltpu.make_async_copy(kz.at[ahead], kz.at[ahead], k_recv.at[2]).wait()
    gram = kz[:NZ].sum(axis=0)

    row = lax.broadcasted_iota(jnp.int32, (NG, 128), 0)
    col = lax.broadcasted_iota(jnp.int32, (NG, 128), 1)
    coef = jnp.ones((NG, 1), F32)
    for level in range(4):
        bit = 1 << level
        diag = jnp.where(row == col, gram, 0.0)
        cross = jnp.where((row ^ bit) == col, gram, 0.0)

        def factor(axis):
            sq = jnp.maximum(jnp.sum(diag, axis=axis, keepdims=True), 0.0)
            return 1.0 - jnp.sum(cross, axis=axis, keepdims=True) / (2.0 * (sq + EPS))

        by_row, by_col = factor(1), factor(0)
        coef = coef * by_row
        gram = gram * by_row * by_col
        gram = gram + jnp.where((row & bit) != 0, pltpu.roll(gram, bit, 0), pltpu.roll(gram, NG - bit, 0))
        gram = gram + jnp.where((col & bit) != 0, pltpu.roll(gram, bit, 1), pltpu.roll(gram, 128 - bit, 1))
    coef = jnp.broadcast_to(coef, (NG, 128))

    def combine(ref):
        width = ref.shape[-1]
        acc = jnp.zeros((ks_rows, width), F32)
        for i in range(NG):
            acc = acc + jnp.tile(coef[i : i + 1], (1, width // 128)) * ref[i].astype(F32)
        return acc

    side = 2 * (g >> 3) - 1

    def home(t):
        dest = (z + (1 + t) * side + 8) & 7
        return remote(zs.at[t], zr.at[t], z_send.at[t], z_recv.at[t], (dest * 2 + core, g))

    for t in (3, 2, 4, 1, 5, 0):
        spread_wait_recv(lr.at[t], lo_recv.at[t])
        zs[t] = combine(lr.at[t]).astype(BF16)
        home(t).start()
    acc = combine(rr)
    for way in range(2):
        par_grad(way).wait_send()
        trail(way).wait_send()
        for t in range(last):
            for h in range(NC):
                hop(t, way, h).wait_send()
    for s in range(NZ):
        for h in range(NC):
            par(s, h).wait_send()
    for t in range(STEPS):
        spread_wait_send(ls.at[t], lo_send.at[t])
    for h in range(NC):
        sent = xs.at[:, :, cols(h)]
        pltpu.make_async_copy(sent, sent, x_send.at[h]).wait()
    spread_wait_send(ps, p_send.at[0])
    pltpu.make_async_copy(kc.at[most], kc.at[most], k_send.at[0]).wait()
    swap.wait_send()
    pltpu.make_async_copy(kz.at[ahead], kz.at[ahead], k_send.at[2]).wait()
    spread_wait_recv(lr.at[last], lo_recv.at[last])
    acc = acc + combine(lr.at[last])
    for t in (0, 5, 1, 4, 2, 3):
        home(t).wait_recv()
        acc = acc + zr[t].astype(F32)
    out_ref[...] = acc
    for t in range(last):
        home(t).wait_send()


def shards(activations, out_grads):
    tok, d = activations.shape
    kv = out_grads.shape[1]
    bw = d // (2 * NZ)
    rows = kv // NG
    dma = pltpu.SemaphoreType.DMA
    grad = pl.pallas_call(
        kernel,
        out_shape=jax.ShapeDtypeStruct((rows, bw), F32),
        in_specs=[pl.BlockSpec(memory_space=pl.ANY)] * 2,
        out_specs=pl.BlockSpec(memory_space=pltpu.VMEM),
        scratch_shapes=[
            pltpu.VMEM((NZ, 2 * tok, bw), BF16),
            pltpu.VMEM((tok, kv), BF16),
            pltpu.VMEM((kv, 2 * tok), BF16),
            pltpu.VMEM((STEPS - 1, 2, kv // 2, bw), BF16),
            pltpu.VMEM((STEPS - 1, 2, kv // 2, bw), BF16),
            pltpu.VMEM((STEPS, NG, rows, bw), BF16),
            pltpu.VMEM((STEPS, NG, rows, bw), BF16),
            pltpu.VMEM((2, kv // 2, bw), BF16),
            pltpu.VMEM((2, kv // 2, bw), BF16),
            pltpu.VMEM((2, kv // 2, bw), F32),
            pltpu.VMEM((NG, rows, bw), BF16),
            pltpu.VMEM((NG, rows, bw), BF16),
            pltpu.VMEM((NG, rows, bw), F32),
            pltpu.VMEM((NG, rows, bw), BF16),
            pltpu.VMEM((NG, rows, bw), BF16),
            pltpu.VMEM((STEPS - 1, rows, bw), BF16),
            pltpu.VMEM((STEPS - 1, rows, bw), BF16),
            pltpu.VMEM((3, NG, 128), F32),
            pltpu.VMEM((NZ + 1, NG, 128), F32),
            pltpu.VMEM((NG, NG, 128), F32),
            dma((NZ + 1,)),
            dma((NZ + 1, 2)),
            dma((NZ + 1, 2)),
            dma((STEPS - 1, 2, NC)),
            dma((STEPS - 1, 2, NC)),
            dma((STEPS,)),
            dma((STEPS,)),
            dma((2,)),
            dma((2,)),
            dma((1,)),
            dma((1,)),
            dma((NC,)),
            dma((NC,)),
            dma((STEPS - 1,)),
            dma((STEPS - 1,)),
            dma((3,)),
            dma((3,)),
            pltpu.SemaphoreType.REGULAR,
            pltpu.SemaphoreType.REGULAR,
        ],
        compiler_params=pltpu.CompilerParams(
            collective_id=0, has_side_effects=True, vmem_limit_bytes=56 << 20
        ),
        cost_estimate=pl.CostEstimate(
            flops=2 * tok * d * kv, bytes_accessed=2 * tok * (d + kv), transcendentals=0
        ),
        name="adasum",
    )(activations, out_grads)
    return grad.T


def solution(mesh):
    placed = (P(("blk", "cube"), None), P(("blk", "cube"), None))
    return jax.shard_map(
        shards, mesh=mesh, in_specs=placed, out_specs=P("blk", "cube"), check_vma=False
    )
```

```python
import jax
import jax.numpy as jnp
from jax import lax
from jax.experimental import pallas as pl
from jax.experimental.pallas import tpu as pltpu
from jax.sharding import PartitionSpec as P

MESH = pl.DeviceIdType.MESH
EPS = 1e-6
NZ = 8
NG = 16
STEPS = NZ - 1
F32, BF16 = jnp.float32, jnp.bfloat16
SLOTS = (7, 1, 6, 2, 0, 5, 3, 4)
CHUNKS = ((0, 256), (256, 256))
NC = len(CHUNKS)


def kernel(
    a_hbm, g_hbm, out_ref,
    av, gv, gt, hs, hr, ls, lr, ts, tr, rest, ps, pr, rr, xs, xr, zs, zr, ks, kz, kc,
    own_sem, par_send, par_recv, hi_send, hi_recv, lo_send, lo_recv, t_send, t_recv,
    p_send, p_recv, x_send, x_recv, z_send, z_recv, k_send, k_recv, near_sem, far_sem,
):
    b = lax.axis_index("blk")
    g = lax.axis_index("cube")
    z, core = b >> 1, b & 1
    y, x = g >> 2, g & 3
    tok = a_hbm.shape[0]
    bw = a_hbm.shape[1] // (2 * NZ)
    kv = g_hbm.shape[1]
    kvh = kv // 2
    ks_rows = kv // NG
    last = STEPS - 1

    def at_plane(dy, dx):
        return (((y + dy) & 3) * 4) + ((x + dx) & 3)

    partner = (b ^ 1, g)
    ring = ((((z + 1) & 7) * 2 + core, g), (((z + 7) & 7) * 2 + core, g))
    plane = [
        at_plane(dy, dx)
        for dy, dx in sorted(
            ((dy, dx) for dy in range(4) for dx in range(4) if dy or dx),
            key=lambda o: -(min(o[0], 4 - o[0]) + min(o[1], 4 - o[1])),
        )
    ]
    line = [(((z + dz) & 7) * 2 + core, g) for dz in (4, 3, 5, 2, 6, 1, 7)]
    beside = [(b, at_plane(dy, dx)) for dy, dx in ((0, 1), (0, 3), (1, 0), (3, 0))]
    across = [(b, at_plane(dy, dx)) for dy, dx in ((0, 2), (2, 0))]

    own = [pltpu.make_async_copy(g_hbm, gv, own_sem.at[NZ])]
    own[0].start()

    barrier = pltpu.get_barrier_semaphore()
    near = [partner, *ring, *beside]
    for p in near:
        pl.semaphore_signal(barrier, inc=1, device_id=p, device_id_type=MESH)

    def block(slot, parity):
        start = (((z + slot) & 7) * 2 + parity) * bw
        return a_hbm.at[:, pl.ds(pl.multiple_of(start, bw), bw)]

    for s in range(NZ):
        own.append(pltpu.make_async_copy(block(s, core), av.at[s, pl.ds(0, tok)], own_sem.at[s]))
    for s in SLOTS[:2]:
        own[s + 1].start()

    own[0].wait()
    gt[:, :tok] = gv[...].T
    pl.semaphore_wait(barrier, len(near))

    def remote(src, dst, send, recv, dev):
        return pltpu.make_async_remote_copy(
            src_ref=src, dst_ref=dst, send_sem=send, recv_sem=recv, device_id=dev, device_id_type=MESH
        )

    def cols(h):
        return pl.ds(*CHUNKS[h])

    def par(slot, h):
        return remote(
            block(slot, 1 - core).at[:, cols(h)], av.at[slot, pl.ds(tok, tok), cols(h)],
            par_send.at[slot, h], par_recv.at[slot, h], partner,
        )

    def par_grad(way):
        rows = pl.ds(way * kvh, kvh)
        return remote(
            gt.at[rows, pl.ds(0, tok)], gt.at[rows, pl.ds(tok, tok)], par_send.at[NZ, way], par_recv.at[NZ, way], partner
        )

    for way in range(2):
        par_grad(way).start()
        par(SLOTS[way], 0).start()

    def fetch(slots):
        for s in slots:
            own[s + 1].start()
            for h in range(NC):
                par(s, h).start()

    for p in beside:
        pl.semaphore_signal(near_sem, inc=1, device_id=p, device_id_type=MESH)

    waited = set()

    def ready(way, slot, h):
        if ("grad", way) not in waited:
            waited.add(("grad", way))
            par_grad(way).wait_recv()
        if slot not in waited:
            waited.add(slot)
            own[slot + 1].wait()
        if (slot, h) not in waited:
            waited.add((slot, h))
            par(slot, h).wait_recv()

    def share(slot, way, h):
        return jnp.dot(
            gt[way * kvh : (way + 1) * kvh, :],
            av[slot, :, cols(h)],
            preferred_element_type=F32,
        )

    def hop(t, way, h):
        return remote(
            hs.at[t, way, :, cols(h)], hr.at[t, way, :, cols(h)], hi_send.at[t, way, h], hi_recv.at[t, way, h], ring[way]
        )

    def trail(way):
        return remote(ts.at[way], tr.at[way], t_send.at[way], t_recv.at[way], ring[way])

    def parts(src, dst, send, recv):
        return [remote(src.at[p], dst.at[g], send, recv, (b, p)) for p in plane] + [
            pltpu.make_async_copy(src.at[g], dst.at[g], recv)
        ]

    def spread(src, dst, send, recv, part):
        for p in plane:
            remote(src.at[p, :, part], dst.at[g, :, part], send, recv, (b, p)).start()
        pltpu.make_async_copy(src.at[g, :, part], dst.at[g, :, part], recv).start()

    def spread_wait_recv(dst, recv):
        pltpu.make_async_copy(dst, dst, recv).wait()

    def spread_wait_send(src, send):
        part = src.at[pl.ds(0, NG - 1)]
        pltpu.make_async_copy(part, part, send).wait()

    def slices(value, h):
        return value.reshape(8, ks_rows, CHUNKS[h][1])

    queue = []
    for t in range(STEPS):
        for h in range(NC):
            for way in range(2):
                if t == 0 and h > 0:
                    par(SLOTS[way], h).start()
            for way in range(2):
                slot = NZ - 1 - t if way == 0 else 1 + t
                mine = slice(way * 8, way * 8 + 8)
                ready(way, slot, h)
                total = share(slot, way, h)
                if t > 0:
                    hop(t - 1, way, h).wait_recv()
                    total = total + hr[t - 1, way, :, cols(h)].astype(F32)
                hi = total.astype(BF16)
                if t < last:
                    hs[t, way, :, cols(h)] = hi
                    hop(t, way, h).start()
                else:
                    xs[mine, :, cols(h)] = slices(hi, h)
                    for p in range(way * 8, way * 8 + 8):
                        remote(
                            xs.at[p, :, cols(h)], xr.at[g, :, cols(h)], x_send.at[h], x_recv.at[h], (ring[way][0], p)
                        ).start()
                lo = (total - hi.astype(F32)).astype(BF16)
                if t < last:
                    ls[t, mine, :, cols(h)] = slices(lo, h)
                else:
                    ts[way, :, cols(h)] = lo
                for copy in queue[:5]:
                    copy.start()
                queue = queue[5:]
        if t == 0:
            fetch(SLOTS[2:5])
            pl.semaphore_wait(near_sem, len(beside))
            for p in across:
                pl.semaphore_signal(far_sem, inc=1, device_id=p, device_id_type=MESH)
            pl.semaphore_wait(far_sem, len(across))
        elif t == 1:
            fetch(SLOTS[5:])
            for h in range(NC):
                for way in range(2):
                    ready(way, 0, h)
                    total = share(0, way, h)
                    hi = total.astype(BF16)
                    ps[way * 8 : way * 8 + 8, :, cols(h)] = slices(hi, h)
                    rest[way, :, cols(h)] = total - hi.astype(F32)
            queue = queue + parts(ps, pr, p_send.at[0], p_recv.at[0])
        if t < last - 1:
            queue = queue + parts(ls.at[t], lr.at[t], lo_send.at[t], lo_recv.at[t])

    gram = None
    spread_wait_recv(pr, p_recv.at[0])
    for h in range(NC):
        spread_wait_recv(xr.at[:, :, cols(h)], x_recv.at[h])
        whole = xr[:, :, cols(h)].astype(F32) + pr[:, :, cols(h)].astype(F32)
        rr[:, :, cols(h)] = whole
        rows = whole.astype(BF16).reshape(kv, CHUNKS[h][1])
        part = lax.dot_general(rows, rows, (((1,), (1,)), ((), ())), preferred_element_type=F32)
        gram = part if gram is None else gram + part
    same = (lax.broadcasted_iota(jnp.int32, (kv, kv), 0) & (ks_rows - 1)) == (
        lax.broadcasted_iota(jnp.int32, (kv, kv), 1) & (ks_rows - 1)
    )
    gram = jnp.where(same, gram, 0.0).reshape(NG, ks_rows, kv).sum(axis=1)
    pick = (lax.broadcasted_iota(jnp.int32, (kv, 128), 0) >> 5) == lax.broadcasted_iota(jnp.int32, (kv, 128), 1)
    gram = jnp.dot(gram, pick.astype(F32), precision=lax.Precision.HIGHEST, preferred_element_type=F32)

    most = pl.ds(0, NG - 1)
    ks[0] = gram
    kc[g] = gram
    for p in plane:
        remote(ks.at[0], kc.at[g], k_send.at[0], k_recv.at[0], (b, p)).start()
    for way in range(2):
        trail(way).start()
    pltpu.make_async_copy(kc.at[most], kc.at[most], k_recv.at[0]).wait()
    gram = kc[...].sum(axis=0)
    ks[1] = gram
    swap = remote(ks.at[1], kz.at[NZ], k_send.at[1], k_recv.at[1], partner)
    swap.start()
    swap.wait_recv()
    gram = gram + kz[NZ]
    ks[2] = gram
    kz[z] = gram
    for p in line:
        remote(ks.at[2], kz.at[z], k_send.at[2], k_recv.at[2], p).start()
    late = last - 1
    spread(ls.at[late], lr.at[late], lo_send.at[late], lo_recv.at[late], slice(None))
    for way in range(2):
        trail(way).wait_recv()
        lo = rest[way] + tr[way].astype(F32)
        ls[last, way * 8 : way * 8 + 8] = lo.astype(BF16).reshape(8, ks_rows, bw)
    spread(ls.at[last], lr.at[last], lo_send.at[last], lo_recv.at[last], slice(None))
    ahead = pl.ds(0, NZ - 1)
    pltpu.make_async_copy(kz.at[ahead], kz.at[ahead], k_recv.at[2]).wait()
    gram = kz[:NZ].sum(axis=0)

    row = lax.broadcasted_iota(jnp.int32, (NG, 128), 0)
    col = lax.broadcasted_iota(jnp.int32, (NG, 128), 1)
    coef = jnp.ones((NG, 1), F32)
    for level in range(4):
        bit = 1 << level
        diag = jnp.where(row == col, gram, 0.0)
        cross = jnp.where((row ^ bit) == col, gram, 0.0)

        def factor(axis):
            sq = jnp.maximum(jnp.sum(diag, axis=axis, keepdims=True), 0.0)
            return 1.0 - jnp.sum(cross, axis=axis, keepdims=True) / (2.0 * (sq + EPS))

        by_row, by_col = factor(1), factor(0)
        coef = coef * by_row
        gram = gram * by_row * by_col
        gram = gram + jnp.where((row & bit) != 0, pltpu.roll(gram, bit, 0), pltpu.roll(gram, NG - bit, 0))
        gram = gram + jnp.where((col & bit) != 0, pltpu.roll(gram, bit, 1), pltpu.roll(gram, 128 - bit, 1))
    coef = jnp.broadcast_to(coef, (NG, 128))

    def combine(ref):
        width = ref.shape[-1]
        acc = jnp.zeros((ks_rows, width), F32)
        for i in range(NG):
            acc = acc + jnp.tile(coef[i : i + 1], (1, width // 128)) * ref[i].astype(F32)
        return acc

    side = 2 * (g >> 3) - 1

    def home(t):
        dest = (z + (1 + t) * side + 8) & 7
        return remote(zs.at[t], zr.at[t], z_send.at[t], z_recv.at[t], (dest * 2 + core, g))

    for t in (3, 2, 4, 1, 0, 5):
        spread_wait_recv(lr.at[t], lo_recv.at[t])
        zs[t] = combine(lr.at[t]).astype(BF16)
        home(t).start()
    acc = combine(rr)
    for way in range(2):
        par_grad(way).wait_send()
        trail(way).wait_send()
        for t in range(last):
            for h in range(NC):
                hop(t, way, h).wait_send()
    for s in range(NZ):
        for h in range(NC):
            par(s, h).wait_send()
    for t in range(STEPS):
        spread_wait_send(ls.at[t], lo_send.at[t])
    for h in range(NC):
        sent = xs.at[:, :, cols(h)]
        pltpu.make_async_copy(sent, sent, x_send.at[h]).wait()
    spread_wait_send(ps, p_send.at[0])
    pltpu.make_async_copy(kc.at[most], kc.at[most], k_send.at[0]).wait()
    swap.wait_send()
    pltpu.make_async_copy(kz.at[ahead], kz.at[ahead], k_send.at[2]).wait()
    spread_wait_recv(lr.at[last], lo_recv.at[last])
    acc = acc + combine(lr.at[last])
    for t in (0, 5, 1, 4, 2, 3):
        home(t).wait_recv()
        acc = acc + zr[t].astype(F32)
    out_ref[...] = acc
    for t in range(last):
        home(t).wait_send()


def shards(activations, out_grads):
    tok, d = activations.shape
    kv = out_grads.shape[1]
    bw = d // (2 * NZ)
    rows = kv // NG
    dma = pltpu.SemaphoreType.DMA
    grad = pl.pallas_call(
        kernel,
        out_shape=jax.ShapeDtypeStruct((rows, bw), F32),
        in_specs=[pl.BlockSpec(memory_space=pl.ANY)] * 2,
        out_specs=pl.BlockSpec(memory_space=pltpu.VMEM),
        scratch_shapes=[
            pltpu.VMEM((NZ, 2 * tok, bw), BF16),
            pltpu.VMEM((tok, kv), BF16),
            pltpu.VMEM((kv, 2 * tok), BF16),
            pltpu.VMEM((STEPS - 1, 2, kv // 2, bw), BF16),
            pltpu.VMEM((STEPS - 1, 2, kv // 2, bw), BF16),
            pltpu.VMEM((STEPS, NG, rows, bw), BF16),
            pltpu.VMEM((STEPS, NG, rows, bw), BF16),
            pltpu.VMEM((2, kv // 2, bw), BF16),
            pltpu.VMEM((2, kv // 2, bw), BF16),
            pltpu.VMEM((2, kv // 2, bw), F32),
            pltpu.VMEM((NG, rows, bw), BF16),
            pltpu.VMEM((NG, rows, bw), BF16),
            pltpu.VMEM((NG, rows, bw), F32),
            pltpu.VMEM((NG, rows, bw), BF16),
            pltpu.VMEM((NG, rows, bw), BF16),
            pltpu.VMEM((STEPS - 1, rows, bw), BF16),
            pltpu.VMEM((STEPS - 1, rows, bw), BF16),
            pltpu.VMEM((3, NG, 128), F32),
            pltpu.VMEM((NZ + 1, NG, 128), F32),
            pltpu.VMEM((NG, NG, 128), F32),
            dma((NZ + 1,)),
            dma((NZ + 1, 2)),
            dma((NZ + 1, 2)),
            dma((STEPS - 1, 2, NC)),
            dma((STEPS - 1, 2, NC)),
            dma((STEPS,)),
            dma((STEPS,)),
            dma((2,)),
            dma((2,)),
            dma((1,)),
            dma((1,)),
            dma((NC,)),
            dma((NC,)),
            dma((STEPS - 1,)),
            dma((STEPS - 1,)),
            dma((3,)),
            dma((3,)),
            pltpu.SemaphoreType.REGULAR,
            pltpu.SemaphoreType.REGULAR,
        ],
        compiler_params=pltpu.CompilerParams(
            collective_id=0, has_side_effects=True, vmem_limit_bytes=56 << 20
        ),
        cost_estimate=pl.CostEstimate(
            flops=2 * tok * d * kv, bytes_accessed=2 * tok * (d + kv), transcendentals=0
        ),
        name="adasum",
    )(activations, out_grads)
    return grad.T


def solution(mesh):
    placed = (P(("blk", "cube"), None), P(("blk", "cube"), None))
    return jax.shard_map(
        shards, mesh=mesh, in_specs=placed, out_specs=P("blk", "cube"), check_vma=False
    )
```

```python
import jax
import jax.numpy as jnp
from jax import lax
from jax.experimental import pallas as pl
from jax.experimental.pallas import tpu as pltpu
from jax.sharding import PartitionSpec as P

MESH = pl.DeviceIdType.MESH
EPS = 1e-6
NZ = 8
NG = 16
STEPS = NZ - 1
F32, BF16 = jnp.float32, jnp.bfloat16
SLOTS = (7, 1, 6, 2, 0, 5, 3, 4)
CHUNKS = ((0, 256), (256, 256))
NC = len(CHUNKS)


def kernel(
    a_hbm, g_hbm, out_ref,
    av, gv, gt, hs, hr, ls, lr, ts, tr, rest, ps, pr, rr, xs, xr, zs, zr, ks, kz, kc,
    own_sem, par_send, par_recv, hi_send, hi_recv, lo_send, lo_recv, t_send, t_recv,
    p_send, p_recv, x_send, x_recv, z_send, z_recv, k_send, k_recv, near_sem, far_sem,
):
    b = lax.axis_index("blk")
    g = lax.axis_index("cube")
    z, core = b >> 1, b & 1
    y, x = g >> 2, g & 3
    tok = a_hbm.shape[0]
    bw = a_hbm.shape[1] // (2 * NZ)
    kv = g_hbm.shape[1]
    kvh = kv // 2
    ks_rows = kv // NG
    last = STEPS - 1

    def at_plane(dy, dx):
        return (((y + dy) & 3) * 4) + ((x + dx) & 3)

    partner = (b ^ 1, g)
    ring = ((((z + 1) & 7) * 2 + core, g), (((z + 7) & 7) * 2 + core, g))
    plane = [
        at_plane(dy, dx)
        for dy, dx in sorted(
            ((dy, dx) for dy in range(4) for dx in range(4) if dy or dx),
            key=lambda o: -(min(o[0], 4 - o[0]) + min(o[1], 4 - o[1])),
        )
    ]
    line = [(((z + dz) & 7) * 2 + core, g) for dz in (4, 3, 5, 2, 6, 1, 7)]
    beside = [(b, at_plane(dy, dx)) for dy, dx in ((0, 1), (0, 3), (1, 0), (3, 0))]
    across = [(b, at_plane(dy, dx)) for dy, dx in ((0, 2), (2, 0))]

    own = [pltpu.make_async_copy(g_hbm, gv, own_sem.at[NZ])]
    own[0].start()

    barrier = pltpu.get_barrier_semaphore()
    near = [partner, *ring, *beside]
    for p in near:
        pl.semaphore_signal(barrier, inc=1, device_id=p, device_id_type=MESH)

    def block(slot, parity):
        start = (((z + slot) & 7) * 2 + parity) * bw
        return a_hbm.at[:, pl.ds(pl.multiple_of(start, bw), bw)]

    for s in range(NZ):
        own.append(pltpu.make_async_copy(block(s, core), av.at[s, pl.ds(0, tok)], own_sem.at[s]))
    for s in SLOTS[:2]:
        own[s + 1].start()

    own[0].wait()
    gt[:, :tok] = gv[...].T
    pl.semaphore_wait(barrier, len(near))

    def remote(src, dst, send, recv, dev):
        return pltpu.make_async_remote_copy(
            src_ref=src, dst_ref=dst, send_sem=send, recv_sem=recv, device_id=dev, device_id_type=MESH
        )

    def cols(h):
        return pl.ds(*CHUNKS[h])

    def par(slot, h):
        return remote(
            block(slot, 1 - core).at[:, cols(h)], av.at[slot, pl.ds(tok, tok), cols(h)],
            par_send.at[slot, h], par_recv.at[slot, h], partner,
        )

    def par_grad(way):
        rows = pl.ds(way * kvh, kvh)
        return remote(
            gt.at[rows, pl.ds(0, tok)], gt.at[rows, pl.ds(tok, tok)], par_send.at[NZ, way], par_recv.at[NZ, way], partner
        )

    for way in range(2):
        par_grad(way).start()
        par(SLOTS[way], 0).start()

    def fetch(slots):
        for s in slots:
            own[s + 1].start()
            for h in range(NC):
                par(s, h).start()

    for p in beside:
        pl.semaphore_signal(near_sem, inc=1, device_id=p, device_id_type=MESH)

    waited = set()

    def ready(way, slot, h):
        if ("grad", way) not in waited:
            waited.add(("grad", way))
            par_grad(way).wait_recv()
        if slot not in waited:
            waited.add(slot)
            own[slot + 1].wait()
        if (slot, h) not in waited:
            waited.add((slot, h))
            par(slot, h).wait_recv()

    def share(slot, way, h):
        return jnp.dot(
            gt[way * kvh : (way + 1) * kvh, :],
            av[slot, :, cols(h)],
            preferred_element_type=F32,
        )

    def hop(t, way, h):
        return remote(
            hs.at[t, way, :, cols(h)], hr.at[t, way, :, cols(h)], hi_send.at[t, way, h], hi_recv.at[t, way, h], ring[way]
        )

    def trail(way):
        return remote(ts.at[way], tr.at[way], t_send.at[way], t_recv.at[way], ring[way])

    def parts(src, dst, send, recv):
        return [remote(src.at[p], dst.at[g], send, recv, (b, p)) for p in plane] + [
            pltpu.make_async_copy(src.at[g], dst.at[g], recv)
        ]

    def spread(src, dst, send, recv, part):
        for p in plane:
            remote(src.at[p, :, part], dst.at[g, :, part], send, recv, (b, p)).start()
        pltpu.make_async_copy(src.at[g, :, part], dst.at[g, :, part], recv).start()

    def spread_wait_recv(dst, recv):
        pltpu.make_async_copy(dst, dst, recv).wait()

    def spread_wait_send(src, send):
        part = src.at[pl.ds(0, NG - 1)]
        pltpu.make_async_copy(part, part, send).wait()

    def slices(value, h):
        return value.reshape(8, ks_rows, CHUNKS[h][1])

    queue = []
    for t in range(STEPS):
        for h in range(NC):
            for way in range(2):
                if t == 0 and h > 0:
                    par(SLOTS[way], h).start()
            for way in range(2):
                slot = NZ - 1 - t if way == 0 else 1 + t
                mine = slice(way * 8, way * 8 + 8)
                ready(way, slot, h)
                total = share(slot, way, h)
                if t > 0:
                    hop(t - 1, way, h).wait_recv()
                    total = total + hr[t - 1, way, :, cols(h)].astype(F32)
                hi = total.astype(BF16)
                if t < last:
                    hs[t, way, :, cols(h)] = hi
                    hop(t, way, h).start()
                else:
                    xs[mine, :, cols(h)] = slices(hi, h)
                    for i in range(8):
                        p = way * 8 + ((g + i) & 7)
                        remote(
                            xs.at[p, :, cols(h)], xr.at[g, :, cols(h)], x_send.at[h], x_recv.at[h], (ring[way][0], p)
                        ).start()
                lo = (total - hi.astype(F32)).astype(BF16)
                if t < last:
                    ls[t, mine, :, cols(h)] = slices(lo, h)
                else:
                    ts[way, :, cols(h)] = lo
                for copy in queue[:5]:
                    copy.start()
                queue = queue[5:]
        if t == 0:
            fetch(SLOTS[2:5])
            pl.semaphore_wait(near_sem, len(beside))
            for p in across:
                pl.semaphore_signal(far_sem, inc=1, device_id=p, device_id_type=MESH)
            pl.semaphore_wait(far_sem, len(across))
        elif t == 1:
            fetch(SLOTS[5:])
            for h in range(NC):
                for way in range(2):
                    ready(way, 0, h)
                    total = share(0, way, h)
                    hi = total.astype(BF16)
                    ps[way * 8 : way * 8 + 8, :, cols(h)] = slices(hi, h)
                    rest[way, :, cols(h)] = total - hi.astype(F32)
            queue = queue + parts(ps, pr, p_send.at[0], p_recv.at[0])
        if t < last - 1:
            queue = queue + parts(ls.at[t], lr.at[t], lo_send.at[t], lo_recv.at[t])

    gram = None
    spread_wait_recv(pr, p_recv.at[0])
    for h in range(NC):
        spread_wait_recv(xr.at[:, :, cols(h)], x_recv.at[h])
        whole = xr[:, :, cols(h)].astype(F32) + pr[:, :, cols(h)].astype(F32)
        rr[:, :, cols(h)] = whole
        rows = whole.astype(BF16).reshape(kv, CHUNKS[h][1])
        part = lax.dot_general(rows, rows, (((1,), (1,)), ((), ())), preferred_element_type=F32)
        gram = part if gram is None else gram + part
    same = (lax.broadcasted_iota(jnp.int32, (kv, kv), 0) & (ks_rows - 1)) == (
        lax.broadcasted_iota(jnp.int32, (kv, kv), 1) & (ks_rows - 1)
    )
    gram = jnp.where(same, gram, 0.0).reshape(NG, ks_rows, kv).sum(axis=1)
    pick = (lax.broadcasted_iota(jnp.int32, (kv, 128), 0) >> 5) == lax.broadcasted_iota(jnp.int32, (kv, 128), 1)
    gram = jnp.dot(gram, pick.astype(F32), precision=lax.Precision.HIGHEST, preferred_element_type=F32)

    most = pl.ds(0, NG - 1)
    ks[0] = gram
    kc[g] = gram
    for p in plane:
        remote(ks.at[0], kc.at[g], k_send.at[0], k_recv.at[0], (b, p)).start()
    for way in range(2):
        trail(way).start()
    pltpu.make_async_copy(kc.at[most], kc.at[most], k_recv.at[0]).wait()
    gram = kc[...].sum(axis=0)
    ks[1] = gram
    swap = remote(ks.at[1], kz.at[NZ], k_send.at[1], k_recv.at[1], partner)
    swap.start()
    swap.wait_recv()
    gram = gram + kz[NZ]
    ks[2] = gram
    kz[z] = gram
    for p in line:
        remote(ks.at[2], kz.at[z], k_send.at[2], k_recv.at[2], p).start()
    late = last - 1
    spread(ls.at[late], lr.at[late], lo_send.at[late], lo_recv.at[late], slice(None))
    for way in range(2):
        trail(way).wait_recv()
        lo = rest[way] + tr[way].astype(F32)
        ls[last, way * 8 : way * 8 + 8] = lo.astype(BF16).reshape(8, ks_rows, bw)
    spread(ls.at[last], lr.at[last], lo_send.at[last], lo_recv.at[last], slice(None))
    ahead = pl.ds(0, NZ - 1)
    pltpu.make_async_copy(kz.at[ahead], kz.at[ahead], k_recv.at[2]).wait()
    gram = kz[:NZ].sum(axis=0)

    row = lax.broadcasted_iota(jnp.int32, (NG, 128), 0)
    col = lax.broadcasted_iota(jnp.int32, (NG, 128), 1)
    coef = jnp.ones((NG, 1), F32)
    for level in range(4):
        bit = 1 << level
        diag = jnp.where(row == col, gram, 0.0)
        cross = jnp.where((row ^ bit) == col, gram, 0.0)

        def factor(axis):
            sq = jnp.maximum(jnp.sum(diag, axis=axis, keepdims=True), 0.0)
            return 1.0 - jnp.sum(cross, axis=axis, keepdims=True) / (2.0 * (sq + EPS))

        by_row, by_col = factor(1), factor(0)
        coef = coef * by_row
        gram = gram * by_row * by_col
        gram = gram + jnp.where((row & bit) != 0, pltpu.roll(gram, bit, 0), pltpu.roll(gram, NG - bit, 0))
        gram = gram + jnp.where((col & bit) != 0, pltpu.roll(gram, bit, 1), pltpu.roll(gram, 128 - bit, 1))
    coef = jnp.broadcast_to(coef, (NG, 128))

    def combine(ref):
        width = ref.shape[-1]
        acc = jnp.zeros((ks_rows, width), F32)
        for i in range(NG):
            acc = acc + jnp.tile(coef[i : i + 1], (1, width // 128)) * ref[i].astype(F32)
        return acc

    side = 2 * (g >> 3) - 1

    def home(t):
        dest = (z + (1 + t) * side + 8) & 7
        return remote(zs.at[t], zr.at[t], z_send.at[t], z_recv.at[t], (dest * 2 + core, g))

    for t in (3, 2, 4, 1, 0, 5):
        spread_wait_recv(lr.at[t], lo_recv.at[t])
        zs[t] = combine(lr.at[t]).astype(BF16)
        home(t).start()
    acc = combine(rr)
    for way in range(2):
        par_grad(way).wait_send()
        trail(way).wait_send()
        for t in range(last):
            for h in range(NC):
                hop(t, way, h).wait_send()
    for s in range(NZ):
        for h in range(NC):
            par(s, h).wait_send()
    for t in range(STEPS):
        spread_wait_send(ls.at[t], lo_send.at[t])
    for h in range(NC):
        sent = xs.at[:, :, cols(h)]
        pltpu.make_async_copy(sent, sent, x_send.at[h]).wait()
    spread_wait_send(ps, p_send.at[0])
    pltpu.make_async_copy(kc.at[most], kc.at[most], k_send.at[0]).wait()
    swap.wait_send()
    pltpu.make_async_copy(kz.at[ahead], kz.at[ahead], k_send.at[2]).wait()
    spread_wait_recv(lr.at[last], lo_recv.at[last])
    acc = acc + combine(lr.at[last])
    for t in (0, 5, 1, 4, 2, 3):
        home(t).wait_recv()
        acc = acc + zr[t].astype(F32)
    out_ref[...] = acc
    for t in range(last):
        home(t).wait_send()


def shards(activations, out_grads):
    tok, d = activations.shape
    kv = out_grads.shape[1]
    bw = d // (2 * NZ)
    rows = kv // NG
    dma = pltpu.SemaphoreType.DMA
    grad = pl.pallas_call(
        kernel,
        out_shape=jax.ShapeDtypeStruct((rows, bw), F32),
        in_specs=[pl.BlockSpec(memory_space=pl.ANY)] * 2,
        out_specs=pl.BlockSpec(memory_space=pltpu.VMEM),
        scratch_shapes=[
            pltpu.VMEM((NZ, 2 * tok, bw), BF16),
            pltpu.VMEM((tok, kv), BF16),
            pltpu.VMEM((kv, 2 * tok), BF16),
            pltpu.VMEM((STEPS - 1, 2, kv // 2, bw), BF16),
            pltpu.VMEM((STEPS - 1, 2, kv // 2, bw), BF16),
            pltpu.VMEM((STEPS, NG, rows, bw), BF16),
            pltpu.VMEM((STEPS, NG, rows, bw), BF16),
            pltpu.VMEM((2, kv // 2, bw), BF16),
            pltpu.VMEM((2, kv // 2, bw), BF16),
            pltpu.VMEM((2, kv // 2, bw), F32),
            pltpu.VMEM((NG, rows, bw), BF16),
            pltpu.VMEM((NG, rows, bw), BF16),
            pltpu.VMEM((NG, rows, bw), F32),
            pltpu.VMEM((NG, rows, bw), BF16),
            pltpu.VMEM((NG, rows, bw), BF16),
            pltpu.VMEM((STEPS - 1, rows, bw), BF16),
            pltpu.VMEM((STEPS - 1, rows, bw), BF16),
            pltpu.VMEM((3, NG, 128), F32),
            pltpu.VMEM((NZ + 1, NG, 128), F32),
            pltpu.VMEM((NG, NG, 128), F32),
            dma((NZ + 1,)),
            dma((NZ + 1, 2)),
            dma((NZ + 1, 2)),
            dma((STEPS - 1, 2, NC)),
            dma((STEPS - 1, 2, NC)),
            dma((STEPS,)),
            dma((STEPS,)),
            dma((2,)),
            dma((2,)),
            dma((1,)),
            dma((1,)),
            dma((NC,)),
            dma((NC,)),
            dma((STEPS - 1,)),
            dma((STEPS - 1,)),
            dma((3,)),
            dma((3,)),
            pltpu.SemaphoreType.REGULAR,
            pltpu.SemaphoreType.REGULAR,
        ],
        compiler_params=pltpu.CompilerParams(
            collective_id=0, has_side_effects=True, vmem_limit_bytes=56 << 20
        ),
        cost_estimate=pl.CostEstimate(
            flops=2 * tok * d * kv, bytes_accessed=2 * tok * (d + kv), transcendentals=0
        ),
        name="adasum",
    )(activations, out_grads)
    return grad.T


def solution(mesh):
    placed = (P(("blk", "cube"), None), P(("blk", "cube"), None))
    return jax.shard_map(
        shards, mesh=mesh, in_specs=placed, out_specs=P("blk", "cube"), check_vma=False
    )
```
